128 devices in a mesh: mem: 32 (over z, y, core), band: 4 (over x).
Axes of the slice: x: 4, y: 4, z: 4, core: 2. Of those that a mesh axis runs over, the one named last changes fastest.
Arguments:
- ensemble: float32 [256, 1024, 256], P('mem', 'band'), may hold values from -8 to 8
- column_operator: float32 [128, 128], replicated, may hold values from -0.5 to 0.5
- patch_order: int32 [4, 256], P('band'), may hold values from 0 to 255, as said below
- obs_index: int32 [4, 256, 512], P('band'), may hold values from 0 to 255
- obs_count: int32 [4, 256], P('band', 'mem'), may hold values from 1 to 512
- obs_values: float32 [4, 256, 512], P('band', 'mem'), may hold values from -8 to 8
- obs_precision: float32 [4, 256, 512], P('band', 'mem'), may hold values from 2 to 50
Outputs:
- analysis: float32 [256, 1024, 256], P('mem', 'band')
- transform: float32 [4, 256, 256, 256], P('band', 'mem')
The draws below stay inside these ranges and needn't reach their ends.
Inputs may be any that keep to these rules, and one draw needn't show every extreme that they name: `patch_order`: each row is a permutation of 0 to 255.
All inputs are finite; a program needn't handle non-finite values.
Results may differ from the reference program's by a relative error of at most 0.0003.
Values sent between devices are 32-bit elements; how exact they have to be, the bound alone decides.
No kernel may reach another device: no remote copies, remote signals or barrier semaphores. Data moves between devices by JAX's collectives and lax.ppermute only.
A program may use at most 64 MiB of HBM per device.

```python
import math
import jax
import jax.numpy as jnp
from jax import lax

K = 256
LEV = 128
NCH = 128
PCOLS = 2
OBS = 512
ITERS = 12
BAND_PATCHES = 256
NPATCH = 1024
PC = 256
CAND = 256
N_BAND = 4


def draw_patch_order(key, part):
    keys = jax.random.split(jax.random.fold_in(key, 11), N_BAND)
    return jax.vmap(lambda single: jax.random.permutation(single, BAND_PATCHES))(keys).astype(jnp.int32)


def draw_obs_count(key, part):
    first, second, third = jax.random.split(jax.random.fold_in(key, 23), 3)
    total = N_BAND * BAND_PATCHES
    top_power = OBS.bit_length() - 1
    powers = jax.random.randint(first, (total,), 0, top_power).astype(jnp.int32)
    lowest = jnp.left_shift(jnp.ones((total,), jnp.int32), powers)
    counts = lowest + jax.random.randint(second, (total,), 0, lowest).astype(jnp.int32)
    spot = jax.random.randint(third, (), 0, total)
    places = jnp.arange(total, dtype=jnp.int32)
    counts = jnp.where(places == spot, OBS, counts)
    counts = jnp.where(places == (spot + 1) % total, 1, counts)
    return counts.reshape(N_BAND, BAND_PATCHES).astype(jnp.int32)


def touch_ends(drawn, key, low, high):
    longest = drawn.shape.index(max(drawn.shape))
    spots = []
    for shift in (0, 1):
        where = [jax.random.randint(jax.random.fold_in(key, axis), (), 0, length) for axis, length in enumerate(drawn.shape)]
        where[longest] = (where[longest] + shift) % drawn.shape[longest]
        spots.append(tuple(where))
    return drawn.at[spots[0]].set(low).at[spots[1]].set(high)


def steps_of(rng, dims, shards, smallest, top_value):
    def one(axis_at, shards_of):
        draws = jax.random.uniform(jax.random.fold_in(jax.random.fold_in(rng, 6), axis_at), (shards_of,), jnp.float32, smallest / len(shards), top_value / len(shards))
        return jnp.repeat(jnp.exp(draws), dims[axis_at] // shards_of).reshape((-1,) + (1,) * (len(dims) - axis_at - 1))

    loudness = one(*shards[0])
    for cut in shards[1:]:
        loudness = loudness * one(*cut)
    return loudness


def gaussian(key, shape, deviation, limit, pieces=(), kind=jnp.bfloat16):
    values = jax.random.normal(key, shape, jnp.float32) * deviation
    if len(pieces) > 0:
        values = steps_of(key, shape, pieces, -0.22, 0.18) * values
    return jnp.clip(values, min=-limit, max=limit).astype(kind)


def setup_inputs(seed: int = 0) -> dict:
    key_of = jax.random.split(jax.random.key(seed), 8)
    ensemble = gaussian(key_of[0], (K, NPATCH, PC), 2.5, 8.0, ((0, 32), (1, 4)), jnp.float32)
    column_operator = jnp.clip(jax.random.uniform(key_of[1], (LEV, NCH), jnp.float32, -0.5, 0.5), -0.5, 0.5)
    patch_order = draw_patch_order(jax.random.fold_in(key_of[7], 71), 0)
    obs_index = touch_ends(jax.random.randint(key_of[3], (N_BAND, BAND_PATCHES, OBS), 0, CAND), jax.random.fold_in(key_of[3], 1), 0, CAND - 1).astype(jnp.int32)
    obs_count = draw_obs_count(jax.random.fold_in(key_of[7], 71), 0)
    obs_values = gaussian(key_of[5], (N_BAND, BAND_PATCHES, OBS), 1.5, 8.0, ((0, 4), (1, 32)), jnp.float32)
    obs_precision = jnp.clip(jnp.exp(math.log(50.0) - 3.218876 * jax.random.uniform(key_of[6], (N_BAND, BAND_PATCHES, OBS), jnp.float32) ** steps_of(key_of[6], (N_BAND, BAND_PATCHES, OBS), ((0, 4), (1, 32)), -0.2, 0.2)), 2.0, 50.0)
    return {"ensemble": ensemble, "column_operator": column_operator, "patch_order": patch_order, "obs_index": obs_index, "obs_count": obs_count, "obs_values": obs_values, "obs_precision": obs_precision}


def analyse(members, column_operator, index, count, values, precision):
    highest = lax.Precision.HIGHEST
    rows = members.shape[0]
    channel_values = jnp.dot(members.reshape(rows * PCOLS, LEV), column_operator, precision=highest).reshape(rows, PCOLS * NCH)
    picks = jnp.broadcast_to(index[None, :], (rows, OBS))
    observed = jnp.take_along_axis(channel_values, picks, axis=1)
    live = (jnp.arange(OBS, dtype=jnp.int32) < count).astype(jnp.float32)
    obs_weight = precision * live
    state_mean = lax.optimization_barrier(jnp.mean(members, axis=0))
    state_pert = members - state_mean
    obs_mean = lax.optimization_barrier(jnp.mean(observed, axis=0))
    obs_pert = observed - obs_mean
    innov = (values - obs_mean) * obs_weight
    gram = jnp.dot(obs_pert * obs_weight, obs_pert.T, precision=highest)
    identity = jnp.eye(rows, dtype=jnp.float32)
    system = gram + (K - 1.0) * identity
    trace_value = jnp.trace(system)
    ymat = system / trace_value
    zmat = identity
    for sweep in range(ITERS):
        turn = 1.5 * identity - 0.5 * jnp.dot(zmat, ymat, precision=highest)
        ymat, zmat = (jnp.dot(ymat, turn, precision=highest), jnp.dot(turn, zmat, precision=highest))
    root = zmat / jnp.sqrt(trace_value)
    spread = math.sqrt(K - 1.0) * root
    projected = jnp.dot(obs_pert, innov, precision=highest)
    mean_weight = jnp.dot(root, jnp.dot(root, projected, precision=highest), precision=highest)
    coef = spread + mean_weight[:, None]
    result = state_mean + jnp.dot(coef.T, state_pert, precision=highest)
    return (spread, result)

def reference(ensemble, column_operator, patch_order, obs_index, obs_count, obs_values, obs_precision):
    bands = jnp.repeat(jnp.arange(N_BAND, dtype=jnp.int32), BAND_PATCHES)
    patch_ids = (bands * BAND_PATCHES + patch_order.reshape(-1)).astype(jnp.int32)

    def one(items):
        pid, index, count, values, precision = items
        members = lax.dynamic_index_in_dim(ensemble, pid, 1, keepdims=False)
        return analyse(members, column_operator, index, count, values, precision)
    spreads, results = lax.map(one, (patch_ids, obs_index.reshape(-1, OBS), obs_count.reshape(-1), obs_values.reshape(-1, OBS), obs_precision.reshape(-1, OBS)))
    analysis = jnp.zeros_like(ensemble).at[:, patch_ids, :].set(jnp.swapaxes(results, 0, 1))
    transform = spreads.reshape(N_BAND, BAND_PATCHES, K, K)
    return (analysis, transform)
```

```python
import functools
import math

import jax
import jax.numpy as jnp
from jax import lax
from jax.experimental import pallas as pl
from jax.experimental.pallas import tpu as pltpu
from jax.sharding import PartitionSpec as P

F = jnp.float32
BF = jnp.bfloat16
CHUNKS = 1
LOCKSTEP = 4
LANES = 128
VMEM = 56 * 2**20


def split(value, pieces):
    out = []
    for _ in range(pieces):
        head = value.astype(BF)
        out.append(head)
        value = value - head.astype(F)
    return out


def dot(left, right):
    return jnp.dot(left, right, preferred_element_type=F)


def dot_t(left, right):
    return lax.dot_general(left, right, (((1,), (1,)), ((), ())), preferred_element_type=F)


def product(left, right, mul=dot):
    low = mul(left[0], right[1]) + mul(left[1], right[0])
    if len(left) == 3:
        low = low + (mul(left[1], right[1]) + (mul(left[0], right[2]) + mul(left[2], right[0])))
    return mul(left[0], right[0]) + low


def gather_kernel(chunks, order, ens, *outs):
    workers, per_chunk, rows, _ = outs[0].shape
    patches = ens.shape[0] // rows
    per_worker = per_chunk * chunks

    def one(worker, carry):
        for slot in range(per_worker):
            patch = order[worker * per_worker + slot]
            outs[slot // per_chunk][worker, slot % per_chunk] = ens[pl.ds(patch, rows, stride=patches), :]
        return carry

    lax.fori_loop(0, workers, one, 0)


def scatter_kernel(chunks, order, *refs):
    ins, out = refs[:-1], refs[-1]
    workers, per_chunk, rows, _ = ins[0].shape
    patches = out.shape[0] // rows
    per_worker = per_chunk * chunks

    def one(worker, carry):
        for slot in range(per_worker):
            patch = order[worker * per_worker + slot]
            out[pl.ds(patch, rows, stride=patches), :] = ins[slot // per_chunk][worker, slot % per_chunk]
        return carry

    lax.fori_loop(0, workers, one, 0)


def slots_kernel(count, index, values, precision, out):
    patches, slots = index.shape
    channels = out.shape[2]
    place = lax.broadcasted_iota(jnp.int32, (channels, slots), 0)
    lane = lax.broadcasted_iota(jnp.int32, (1, slots), 1)
    for p in range(patches):
        weight = jnp.where(lane < count[0, p], precision[p : p + 1, :], 0.0)
        rows = split(weight, 3) + split(weight * values[p : p + 1, :], 3)
        rows = jnp.concatenate([row.astype(F) for row in rows] + [jnp.zeros((2, slots), F)], axis=0).astype(BF)
        picker = jnp.where(place == index[p : p + 1, :], 1.0, 0.0).astype(BF)
        sums = dot_t(rows, picker)
        total = sums[0:1] + (sums[1:2] + sums[2:3])
        valued = sums[3:4] + (sums[4:5] + sums[5:6])
        out[p] = jnp.concatenate([total, jnp.sqrt(total), valued, jnp.zeros((5, channels), F)], axis=0)


def double_poly(mats, pieces):
    parts = [split(m, pieces) for m in mats]
    squares = [product(p[:2], p[:2]) for p in parts]
    outer = [split(s, 2) for s in squares]
    inner = [split(0.0625 * s - 0.5625 * m, 2) for s, m in zip(squares, mats)]
    poly = [
        product(o, i) + (1.6875 * s - 2.4375 * m) for o, i, s, m in zip(outer, inner, squares, mats)
    ]
    return parts, poly


def double_step(mats, roots, pieces):
    parts, poly = double_poly(mats, pieces)
    spoly = [split(p, pieces) for p in poly]
    if roots is None:
        size = mats[0].shape[0]
        row = lax.broadcasted_iota(jnp.int32, (size, size), 0)
        col = lax.broadcasted_iota(jnp.int32, (size, size), 1)
        new_roots = [jnp.where(row == col, p + 2.25, p) for p in poly]
    else:
        new_roots = [2.25 * z + product(split(z, 2), p[:2]) for z, p in zip(roots, spoly)]
    half = [2.25 * m + product(s, p) for m, s, p in zip(mats, parts, spoly)]
    new_mats = [2.25 * u + product(split(u, pieces), p) for u, p in zip(half, spoly)]
    return new_mats, new_roots


def analyse_kernel(members, doubles, state, sums, operator, *refs):
    transform, updated = refs[-2:]
    n = transform.shape[0]
    cells = state.shape[3]
    every = range(n)
    row = lax.broadcasted_iota(jnp.int32, (members, members), 0)
    col = lax.broadcasted_iota(jnp.int32, (members, members), 1)
    inflation = members - 1.0

    oper = split(operator[...], 3)
    mats, traces, projected = [], [], []
    states = [state[:, i].reshape(members, cells) for i in every]
    mapped = [product(split(x, 3), oper) for x in states]
    for i in every:
        mean = jnp.mean(mapped[i], axis=0, keepdims=True)
        pert = mapped[i] - mean
        innov = sums[i, 2:3] - mean * sums[i, 0:1]
        projected.append(jnp.sum(pert * innov, axis=1, keepdims=True))
        scaled = pert * sums[i, 1:2]
        trace = jnp.sum(jnp.sum(scaled * scaled, axis=0, keepdims=True), axis=1, keepdims=True)
        traces.append(trace + inflation * members)
        mats.append(scaled)
    pieces = [split(m, 3) for m in mats]
    grams = [product(p, p, dot_t) for p in pieces]
    mats = [jnp.where(row == col, g + inflation, g) / t for g, t in zip(grams, traces)]

    mats, roots = double_step(mats, None, 3)
    mats, roots = lax.fori_loop(0, doubles - 2, lambda k, c: double_step(c[0], c[1], 2), (mats, roots))
    _, poly = double_poly(mats, 2)
    roots = [2.25 * z + product(split(z, 2), split(p, 2)) for z, p in zip(roots, poly)]

    for i in every:
        root, trace = roots[i], traces[i]
        scale = math.sqrt(inflation) / jnp.sqrt(trace)
        transform[i] = root * scale
        x = state[:, i].reshape(members, cells)
        mean = jnp.mean(x, axis=0, keepdims=True)
        pert = x - mean
        once = jnp.sum(root * projected[i], axis=0, keepdims=True)
        weight = jnp.sum(root * once, axis=1, keepdims=True) / trace
        shift = mean + jnp.sum(pert * weight, axis=0, keepdims=True)
        result = shift + scale * product(split(root, 2), split(pert, 2))
        updated[:, i] = result.reshape(updated.shape[0], updated.shape[2], cells)


def analyse(chunk, chunks, state, sums, operator, transform):
    workers, per_chunk, rows, cells = state.shape
    members = workers * rows
    channels = sums.shape[2]
    n = min(LOCKSTEP, per_chunk)
    steps = per_chunk // n
    first = chunk * steps
    in_specs = [
        pl.BlockSpec((workers, n, rows, cells), lambda i: (0, i, 0, 0)),
        pl.BlockSpec((n, 8, channels), lambda i: (first + i, 0, 0)),
        pl.BlockSpec((cells, channels), lambda i: (0, 0)),
    ]
    args = [state, sums, operator]
    aliases = {}
    if transform is not None:
        in_specs.append(pl.BlockSpec(memory_space=pl.ANY))
        args.append(transform)
        aliases = {3: 0}
    return pl.pallas_call(
        functools.partial(analyse_kernel, members, 6),
        grid=(steps,),
        in_specs=in_specs,
        out_specs=[
            pl.BlockSpec((n, members, members), lambda i: (first + i, 0, 0)),
            pl.BlockSpec((workers, n, rows, cells), lambda i: (0, i, 0, 0)),
        ],
        out_shape=[
            jax.ShapeDtypeStruct((per_chunk * chunks, members, members), F),
            jax.ShapeDtypeStruct(state.shape, F),
        ],
        input_output_aliases=aliases,
        compiler_params=pltpu.CompilerParams(vmem_limit_bytes=VMEM),
        cost_estimate=pl.CostEstimate(
            flops=per_chunk * 100 * 2 * members**3, bytes_accessed=12 * per_chunk * members**2, transcendentals=0
        ),
        name="analyse",
    )(*args)


def local(ensemble, column_operator, patch_order, obs_index, obs_count, obs_values, obs_precision):
    rows, band_patches, cells = ensemble.shape
    workers = lax.axis_size("mem")
    worker = lax.axis_index("mem")
    per_worker = band_patches // workers
    per_chunk = per_worker // CHUNKS
    levels = column_operator.shape[0]
    columns = cells // levels
    channels = columns * column_operator.shape[1]
    smem = pl.BlockSpec(memory_space=pltpu.SMEM)
    vmem = pl.BlockSpec(memory_space=pltpu.VMEM)
    params = pltpu.CompilerParams(vmem_limit_bytes=VMEM)
    piece = jax.ShapeDtypeStruct((workers, per_chunk, rows, cells), F)
    order = patch_order[0]
    lanes = cells // LANES
    strip = pl.BlockSpec((rows * band_patches, LANES), lambda j: (0, j))
    block = pl.BlockSpec((workers, per_chunk, rows, LANES), lambda j: (0, 0, 0, j))

    listed = pl.pallas_call(
        functools.partial(gather_kernel, CHUNKS),
        grid=(lanes,),
        in_specs=[smem, strip],
        out_specs=[block] * CHUNKS,
        out_shape=[piece] * CHUNKS,
        compiler_params=params,
        name="gather",
    )(order, ensemble.reshape(rows * band_patches, cells))

    my_index = lax.dynamic_slice_in_dim(obs_index[0], worker * per_worker, per_worker, 0)
    sums = pl.pallas_call(
        slots_kernel,
        in_specs=[smem, vmem, vmem, vmem],
        out_specs=vmem,
        out_shape=jax.ShapeDtypeStruct((per_worker, 8, channels), F),
        compiler_params=params,
        name="slots",
    )(obs_count, my_index, obs_values[0], obs_precision[0])
    width = column_operator.shape[1]
    operator = jnp.concatenate(
        [jnp.pad(column_operator, ((0, 0), (k * width, channels - (k + 1) * width))) for k in range(columns)]
    )

    transform = None
    returned = []
    states = [lax.all_to_all(x, "mem", 0, 0, tiled=True) for x in listed]
    for c in range(CHUNKS):
        transform, updated = analyse(c, CHUNKS, states[c], sums, operator, transform)
        returned.append(lax.all_to_all(updated, "mem", 0, 0, tiled=True))

    restored = pl.pallas_call(
        functools.partial(scatter_kernel, CHUNKS),
        grid=(lanes,),
        in_specs=[smem] + [block] * CHUNKS,
        out_specs=strip,
        out_shape=jax.ShapeDtypeStruct((rows * band_patches, cells), F),
        compiler_params=params,
        name="scatter",
    )(order, *returned)
    return (restored.reshape(rows, band_patches, cells), transform[None])


def solution(mesh):
    placed = (
        P("mem", "band", None),
        P(),
        P("band", None),
        P("band", None, None),
        P("band", "mem"),
        P("band", "mem", None),
        P("band", "mem", None),
    )
    return jax.shard_map(
        local,
        mesh=mesh,
        in_specs=placed,
        out_specs=(P("mem", "band", None), P("band", "mem", None, None)),
        check_vma=False,
    )
```

```python
import functools
import math

import jax
import jax.numpy as jnp
from jax import lax
from jax.experimental import pallas as pl
from jax.experimental.pallas import tpu as pltpu
from jax.sharding import PartitionSpec as P

F = jnp.float32
BF = jnp.bfloat16
CHUNKS = 2
LOCKSTEP = 4
LANES = 128
VMEM = 56 * 2**20


def split(value, pieces):
    out = []
    for _ in range(pieces):
        head = value.astype(BF)
        out.append(head)
        value = value - head.astype(F)
    return out


def dot(left, right):
    return jnp.dot(left, right, preferred_element_type=F)


def dot_t(left, right):
    return lax.dot_general(left, right, (((1,), (1,)), ((), ())), preferred_element_type=F)


def product(left, right, mul=dot):
    n = left[0].shape[0]
    first = mul(jnp.concatenate(left, axis=0), right[0])
    if len(left) == 2:
        return first[:n] + (first[n:] + mul(left[0], right[1]))
    second = mul(jnp.concatenate(left[:2], axis=0), right[1])
    low = second[n:] + (mul(left[0], right[2]) + first[2 * n :])
    return first[:n] + ((first[n : 2 * n] + second[:n]) + low)


def stacked(left, other, right):
    both = [jnp.concatenate([a, b], axis=0) for a, b in zip(left, other)]
    result = product(both, right)
    n = left[0].shape[0]
    return result[:n], result[n:]


def gather_kernel(chunk, per_worker, order, ens, out):
    workers, per_chunk, rows, _ = out.shape
    patches = ens.shape[0] // rows

    def one(worker, carry):
        for slot in range(per_chunk):
            patch = order[worker * per_worker + chunk * per_chunk + slot]
            out[worker, slot] = ens[pl.ds(patch, rows, stride=patches), :]
        return carry

    lax.fori_loop(0, workers, one, 0)


def scatter_kernel(chunks, order, *refs):
    ins, out = refs[:-1], refs[-1]
    workers, per_chunk, rows, _ = ins[0].shape
    patches = out.shape[0] // rows
    per_worker = per_chunk * chunks

    def one(worker, carry):
        for slot in range(per_worker):
            patch = order[worker * per_worker + slot]
            out[pl.ds(patch, rows, stride=patches), :] = ins[slot // per_chunk][worker, slot % per_chunk]
        return carry

    lax.fori_loop(0, workers, one, 0)


def slots_kernel(count, index, values, precision, out):
    patches, slots = index.shape
    channels = out.shape[2]
    place = lax.broadcasted_iota(jnp.int32, (channels, slots), 0)
    lane = lax.broadcasted_iota(jnp.int32, (1, slots), 1)
    for p in range(patches):
        weight = jnp.where(lane < count[0, p], precision[p : p + 1, :], 0.0)
        rows = split(weight, 3) + split(weight * values[p : p + 1, :], 3)
        rows = jnp.concatenate([row.astype(F) for row in rows] + [jnp.zeros((2, slots), F)], axis=0).astype(BF)
        picker = jnp.where(place == index[p : p + 1, :], 1.0, 0.0).astype(BF)
        sums = dot_t(rows, picker)
        total = sums[0:1] + (sums[1:2] + sums[2:3])
        valued = sums[3:4] + (sums[4:5] + sums[5:6])
        out[p] = jnp.concatenate([total, jnp.sqrt(total), valued, jnp.zeros((5, channels), F)], axis=0)


def double_poly(mats, pieces):
    parts = [split(m, pieces) for m in mats]
    squares = [product(p[:2], p[:2]) for p in parts]
    outer = [split(s, 2) for s in squares]
    inner = [split(0.0625 * s - 0.5625 * m, 2) for s, m in zip(squares, mats)]
    poly = [
        product(o, i) + (1.6875 * s - 2.4375 * m) for o, i, s, m in zip(outer, inner, squares, mats)
    ]
    return parts, poly


def double_step(mats, roots, pieces):
    parts, poly = double_poly(mats, pieces)
    spoly = [split(p, pieces) for p in poly]
    if roots is None:
        size = mats[0].shape[0]
        row = lax.broadcasted_iota(jnp.int32, (size, size), 0)
        col = lax.broadcasted_iota(jnp.int32, (size, size), 1)
        new_roots = [jnp.where(row == col, p + 2.25, p) for p in poly]
        half = [2.25 * m + product(s, p) for m, s, p in zip(mats, parts, spoly)]
    else:
        half, new_roots = [], []
        for m, z, s, p in zip(mats, roots, parts, spoly):
            upper, lower = stacked(s, split(z, 2), p)
            half.append(2.25 * m + upper)
            new_roots.append(2.25 * z + lower)
    new_mats = [2.25 * u + product(split(u, pieces), p) for u, p in zip(half, spoly)]
    return new_mats, new_roots


def analyse_kernel(members, doubles, state, sums, operator, *refs):
    transform, updated = refs[-2:]
    n = transform.shape[0]
    cells = state.shape[3]
    every = range(n)
    row = lax.broadcasted_iota(jnp.int32, (members, members), 0)
    col = lax.broadcasted_iota(jnp.int32, (members, members), 1)
    inflation = members - 1.0

    oper = split(operator[...], 3)
    mats, traces, projected = [], [], []
    states = [state[:, i].reshape(members, cells) for i in every]
    mapped = [product(split(x, 3), oper) for x in states]
    for i in every:
        mean = jnp.mean(mapped[i], axis=0, keepdims=True)
        pert = mapped[i] - mean
        innov = sums[i, 2:3] - mean * sums[i, 0:1]
        projected.append(jnp.sum(pert * innov, axis=1, keepdims=True))
        scaled = pert * sums[i, 1:2]
        trace = jnp.sum(jnp.sum(scaled * scaled, axis=0, keepdims=True), axis=1, keepdims=True)
        traces.append(trace + inflation * members)
        mats.append(scaled)
    pieces = [split(m, 3) for m in mats]
    grams = [product(p, p, dot_t) for p in pieces]
    mats = [jnp.where(row == col, g + inflation, g) / t for g, t in zip(grams, traces)]

    mats, roots = double_step(mats, None, 3)
    for _ in range(doubles - 2):
        mats, roots = double_step(mats, roots, 2)
    _, poly = double_poly(mats, 2)
    roots = [2.25 * z + product(split(z, 2), split(p, 2)) for z, p in zip(roots, poly)]

    for i in every:
        root, trace = roots[i], traces[i]
        scale = math.sqrt(inflation) / jnp.sqrt(trace)
        transform[i] = root * scale
        x = state[:, i].reshape(members, cells)
        mean = jnp.mean(x, axis=0, keepdims=True)
        pert = x - mean
        once = jnp.sum(root * projected[i], axis=0, keepdims=True)
        weight = jnp.sum(root * once, axis=1, keepdims=True) / trace
        shift = mean + jnp.sum(pert * weight, axis=0, keepdims=True)
        result = shift + scale * product(split(root, 2), split(pert, 2))
        updated[:, i] = result.reshape(updated.shape[0], updated.shape[2], cells)


def analyse(chunk, chunks, state, sums, operator, transform):
    workers, per_chunk, rows, cells = state.shape
    members = workers * rows
    channels = sums.shape[2]
    n = min(LOCKSTEP, per_chunk)
    steps = per_chunk // n
    first = chunk * steps
    in_specs = [
        pl.BlockSpec((workers, n, rows, cells), lambda i: (0, i, 0, 0)),
        pl.BlockSpec((n, 8, channels), lambda i: (first + i, 0, 0)),
        pl.BlockSpec((cells, channels), lambda i: (0, 0)),
    ]
    args = [state, sums, operator]
    aliases = {}
    if transform is not None:
        in_specs.append(pl.BlockSpec(memory_space=pl.ANY))
        args.append(transform)
        aliases = {3: 0}
    return pl.pallas_call(
        functools.partial(analyse_kernel, members, 6),
        grid=(steps,),
        in_specs=in_specs,
        out_specs=[
            pl.BlockSpec((n, members, members), lambda i: (first + i, 0, 0)),
            pl.BlockSpec((workers, n, rows, cells), lambda i: (0, i, 0, 0)),
        ],
        out_shape=[
            jax.ShapeDtypeStruct((per_chunk * chunks, members, members), F),
            jax.ShapeDtypeStruct(state.shape, F),
        ],
        input_output_aliases=aliases,
        compiler_params=pltpu.CompilerParams(vmem_limit_bytes=VMEM),
        cost_estimate=pl.CostEstimate(
            flops=per_chunk * 100 * 2 * members**3, bytes_accessed=12 * per_chunk * members**2, transcendentals=0
        ),
        name="analyse",
    )(*args)


def local(ensemble, column_operator, patch_order, obs_index, obs_count, obs_values, obs_precision):
    rows, band_patches, cells = ensemble.shape
    workers = lax.axis_size("mem")
    worker = lax.axis_index("mem")
    per_worker = band_patches // workers
    per_chunk = per_worker // CHUNKS
    levels = column_operator.shape[0]
    columns = cells // levels
    channels = columns * column_operator.shape[1]
    smem = pl.BlockSpec(memory_space=pltpu.SMEM)
    vmem = pl.BlockSpec(memory_space=pltpu.VMEM)
    params = pltpu.CompilerParams(vmem_limit_bytes=VMEM)
    piece = jax.ShapeDtypeStruct((workers, per_chunk, rows, cells), F)
    order = patch_order[0]
    lanes = cells // LANES
    strip = pl.BlockSpec((rows * band_patches, LANES), lambda j: (0, j))
    block = pl.BlockSpec((workers, per_chunk, rows, LANES), lambda j: (0, 0, 0, j))

    listed = [
        pl.pallas_call(
            functools.partial(gather_kernel, c, per_worker),
            grid=(lanes,),
            in_specs=[smem, strip],
            out_specs=block,
            out_shape=piece,
            compiler_params=params,
            cost_estimate=pl.CostEstimate(flops=0, bytes_accessed=2 * ensemble.size * 4, transcendentals=0),
            name="gather",
        )(order, ensemble.reshape(rows * band_patches, cells))
        for c in range(CHUNKS)
    ]

    my_index = lax.dynamic_slice_in_dim(obs_index[0], worker * per_worker, per_worker, 0)
    sums = pl.pallas_call(
        slots_kernel,
        in_specs=[smem, vmem, vmem, vmem],
        out_specs=vmem,
        out_shape=jax.ShapeDtypeStruct((per_worker, 8, channels), F),
        compiler_params=params,
        name="slots",
    )(obs_count, my_index, obs_values[0], obs_precision[0])
    width = column_operator.shape[1]
    operator = jnp.concatenate(
        [jnp.pad(column_operator, ((0, 0), (k * width, channels - (k + 1) * width))) for k in range(columns)]
    )

    transform = None
    returned = []
    states = [lax.all_to_all(x, "mem", 0, 0, tiled=True) for x in listed]
    for c in range(CHUNKS):
        transform, updated = analyse(c, CHUNKS, states[c], sums, operator, transform)
        returned.append(lax.all_to_all(updated, "mem", 0, 0, tiled=True))

    restored = pl.pallas_call(
        functools.partial(scatter_kernel, CHUNKS),
        grid=(lanes,),
        in_specs=[smem] + [block] * CHUNKS,
        out_specs=strip,
        out_shape=jax.ShapeDtypeStruct((rows * band_patches, cells), F),
        compiler_params=params,
        name="scatter",
    )(order, *returned)
    return (restored.reshape(rows, band_patches, cells), transform[None])


def solution(mesh):
    placed = (
        P("mem", "band", None),
        P(),
        P("band", None),
        P("band", None, None),
        P("band", "mem"),
        P("band", "mem", None),
        P("band", "mem", None),
    )
    return jax.shard_map(
        local,
        mesh=mesh,
        in_specs=placed,
        out_specs=(P("mem", "band", None), P("band", "mem", None, None)),
        check_vma=False,
    )
```

```python
import functools
import math

import jax
import jax.numpy as jnp
from jax import lax
from jax.experimental import pallas as pl
from jax.experimental.pallas import tpu as pltpu
from jax.sharding import PartitionSpec as P

F = jnp.float32
BF = jnp.bfloat16
CHUNKS = 2
ANALYSE_VMEM = 40 * 2**20
LANES = 128
VMEM = 56 * 2**20


def split(value, pieces):
    out = []
    for _ in range(pieces):
        head = value.astype(BF)
        out.append(head)
        value = value - head.astype(F)
    return out


def dot(left, right):
    return jnp.dot(left, right, preferred_element_type=F)


def dot_t(left, right):
    return lax.dot_general(left, right, (((1,), (1,)), ((), ())), preferred_element_type=F)


def product(left, right, mul=dot):
    n = left[0].shape[0]
    first = mul(jnp.concatenate(left, axis=0), right[0])
    if len(left) == 2:
        return first[:n] + (first[n:] + mul(left[0], right[1]))
    second = mul(jnp.concatenate(left[:2], axis=0), right[1])
    low = second[n:] + (mul(left[0], right[2]) + first[2 * n :])
    return first[:n] + ((first[n : 2 * n] + second[:n]) + low)


def stacked(left, other, right):
    both = [jnp.concatenate([a, b], axis=0) for a, b in zip(left, other)]
    result = product(both, right)
    n = left[0].shape[0]
    return result[:n], result[n:]


def gather_kernel(chunk, per_worker, order, ens, out):
    workers, per_chunk, rows, _ = out.shape
    patches = ens.shape[0] // rows

    def one(worker, carry):
        for slot in range(per_chunk):
            patch = order[worker * per_worker + chunk * per_chunk + slot]
            out[worker, slot] = ens[pl.ds(patch, rows, stride=patches), :]
        return carry

    lax.fori_loop(0, workers, one, 0, unroll=4)


def scatter_kernel(chunks, order, *refs):
    ins, out = refs[:-1], refs[-1]
    workers, per_chunk, rows, _ = ins[0].shape
    patches = out.shape[0] // rows
    per_worker = per_chunk * chunks

    def one(worker, carry):
        for slot in range(per_worker):
            patch = order[worker * per_worker + slot]
            out[pl.ds(patch, rows, stride=patches), :] = ins[slot // per_chunk][worker, slot % per_chunk]
        return carry

    lax.fori_loop(0, workers, one, 0, unroll=4)


def slots_kernel(count, index, values, precision, out):
    patches, slots = index.shape
    channels = out.shape[2]
    place = lax.broadcasted_iota(jnp.int32, (channels, slots), 0)
    lane = lax.broadcasted_iota(jnp.int32, (1, slots), 1)
    for p in range(patches):
        weight = jnp.where(lane < count[0, p], precision[p : p + 1, :], 0.0)
        rows = split(weight, 3) + split(weight * values[p : p + 1, :], 3)
        rows = jnp.concatenate([row.astype(F) for row in rows] + [jnp.zeros((2, slots), F)], axis=0).astype(BF)
        picker = jnp.where(place == index[p : p + 1, :], 1.0, 0.0).astype(BF)
        sums = dot_t(rows, picker)
        total = sums[0:1] + (sums[1:2] + sums[2:3])
        valued = sums[3:4] + (sums[4:5] + sums[5:6])
        out[p] = jnp.concatenate([total, jnp.sqrt(total), valued, jnp.zeros((5, channels), F)], axis=0)


def double_poly(mats, pieces):
    parts = [split(m, pieces) for m in mats]
    squares = [product(p[:2], p[:2]) for p in parts]
    outer = [split(s, 2) for s in squares]
    inner = [split(0.0625 * s - 0.5625 * m, 2) for s, m in zip(squares, mats)]
    poly = [
        product(o, i) + (1.6875 * s - 2.4375 * m) for o, i, s, m in zip(outer, inner, squares, mats)
    ]
    return parts, poly


def double_step(mats, roots, pieces):
    parts, poly = double_poly(mats, pieces)
    spoly = [split(p, pieces) for p in poly]
    if roots is None:
        size = mats[0].shape[0]
        row = lax.broadcasted_iota(jnp.int32, (size, size), 0)
        col = lax.broadcasted_iota(jnp.int32, (size, size), 1)
        new_roots = [jnp.where(row == col, p + 2.25, p) for p in poly]
        half = [2.25 * m + product(s, p) for m, s, p in zip(mats, parts, spoly)]
    else:
        half, new_roots = [], []
        for m, z, s, p in zip(mats, roots, parts, spoly):
            upper, lower = stacked(s, split(z, 2), p)
            half.append(2.25 * m + upper)
            new_roots.append(2.25 * z + lower)
    new_mats = [2.25 * u + product(split(u, pieces), p) for u, p in zip(half, spoly)]
    return new_mats, new_roots


def analyse_kernel(members, doubles, first, state, sums, operator, *refs):
    transform_out, updated, transform, leave = refs[-4:]
    n = transform.shape[0]
    cells = state.shape[3]
    every = range(n)
    row = lax.broadcasted_iota(jnp.int32, (members, members), 0)
    col = lax.broadcasted_iota(jnp.int32, (members, members), 1)
    inflation = members - 1.0

    oper = split(operator[...], 3)
    mats, traces, projected = [], [], []
    states = [state[:, i].reshape(members, cells) for i in every]
    mapped = [product(split(x, 3), oper) for x in states]
    for i in every:
        mean = jnp.mean(mapped[i], axis=0, keepdims=True)
        pert = mapped[i] - mean
        innov = sums[first + i, 2:3] - mean * sums[first + i, 0:1]
        projected.append(jnp.sum(pert * innov, axis=1, keepdims=True))
        scaled = pert * sums[first + i, 1:2]
        trace = jnp.sum(jnp.sum(scaled * scaled, axis=0, keepdims=True), axis=1, keepdims=True)
        traces.append(trace + inflation * members)
        mats.append(scaled)
    pieces = [split(m, 3) for m in mats]
    grams = [product(p, p, dot_t) for p in pieces]
    mats = [jnp.where(row == col, g + inflation, g) * (1.0 / t) for g, t in zip(grams, traces)]

    mats, roots = double_step(mats, None, 3)
    for _ in range(doubles - 2):
        mats, roots = double_step(mats, roots, 2)
    _, poly = double_poly(mats, 2)
    roots = [2.25 * z + product(split(z, 2), split(p, 2)) for z, p in zip(roots, poly)]

    for i in every:
        root, trace = roots[i], traces[i]
        scale = math.sqrt(inflation) / jnp.sqrt(trace)
        transform[i] = root * scale
        x = state[:, i].reshape(members, cells)
        mean = jnp.mean(x, axis=0, keepdims=True)
        pert = x - mean
        once = jnp.sum(root * projected[i], axis=0, keepdims=True)
        weight = jnp.sum(root * once, axis=1, keepdims=True) / trace
        shift = mean + jnp.sum(pert * weight, axis=0, keepdims=True)
        result = shift + scale * product(split(root, 2), split(pert, 2))
        updated[:, i] = result.reshape(updated.shape[0], updated.shape[2], cells)
    copy = pltpu.make_async_copy(transform, transform_out.at[pl.ds(first, n)], leave)
    copy.start()
    copy.wait()


def analyse(chunk, chunks, state, sums, operator, transform):
    workers, per_chunk, rows, cells = state.shape
    members = workers * rows
    anywhere = pl.BlockSpec(memory_space=pl.ANY)
    vmem = pl.BlockSpec(memory_space=pltpu.VMEM)
    first = chunk * per_chunk
    in_specs = [vmem, vmem, vmem]
    args = [pltpu.with_memory_space_constraint(state, pltpu.VMEM), sums, operator]
    aliases = {}
    if transform is not None:
        in_specs.append(anywhere)
        args.append(transform)
        aliases = {3: 0}
    return pl.pallas_call(
        functools.partial(analyse_kernel, members, 6, first),
        in_specs=in_specs,
        out_specs=[anywhere, vmem],
        out_shape=[
            jax.ShapeDtypeStruct((per_chunk * chunks, members, members), F),
            pltpu.VMEM(state.shape, F),
        ],
        scratch_shapes=[pltpu.VMEM((per_chunk, members, members), F), pltpu.SemaphoreType.DMA],
        input_output_aliases=aliases,
        compiler_params=pltpu.CompilerParams(vmem_limit_bytes=ANALYSE_VMEM),
        cost_estimate=pl.CostEstimate(
            flops=per_chunk * 100 * 2 * members**3, bytes_accessed=12 * per_chunk * members**2, transcendentals=0
        ),
        name="analyse",
    )(*args)


def local(ensemble, column_operator, patch_order, obs_index, obs_count, obs_values, obs_precision):
    rows, band_patches, cells = ensemble.shape
    workers = lax.axis_size("mem")
    worker = lax.axis_index("mem")
    per_worker = band_patches // workers
    per_chunk = per_worker // CHUNKS
    levels = column_operator.shape[0]
    columns = cells // levels
    channels = columns * column_operator.shape[1]
    smem = pl.BlockSpec(memory_space=pltpu.SMEM)
    vmem = pl.BlockSpec(memory_space=pltpu.VMEM)
    params = pltpu.CompilerParams(vmem_limit_bytes=VMEM)
    piece = jax.ShapeDtypeStruct((workers, per_chunk, rows, cells), F)
    order = patch_order[0]
    lanes = cells // LANES
    strip = pl.BlockSpec((rows * band_patches, LANES), lambda j: (0, j))
    block = pl.BlockSpec((workers, per_chunk, rows, LANES), lambda j: (0, 0, 0, j))

    listed = [
        pl.pallas_call(
            functools.partial(gather_kernel, c, per_worker),
            grid=(lanes,),
            in_specs=[smem, strip],
            out_specs=block,
            out_shape=piece,
            compiler_params=params,
            cost_estimate=pl.CostEstimate(flops=0, bytes_accessed=2 * ensemble.size * 4, transcendentals=0),
            name="gather",
        )(order, ensemble.reshape(rows * band_patches, cells))
        for c in range(CHUNKS)
    ]

    my_index = lax.dynamic_slice_in_dim(obs_index[0], worker * per_worker, per_worker, 0)
    sums = pl.pallas_call(
        slots_kernel,
        in_specs=[smem, vmem, vmem, vmem],
        out_specs=vmem,
        out_shape=jax.ShapeDtypeStruct((per_worker, 8, channels), F),
        compiler_params=params,
        name="slots",
    )(obs_count, my_index, obs_values[0], obs_precision[0])
    width = column_operator.shape[1]
    operator = jnp.concatenate(
        [jnp.pad(column_operator, ((0, 0), (k * width, channels - (k + 1) * width))) for k in range(columns)]
    )

    transform = None
    returned = []
    states = [lax.all_to_all(x, "mem", 0, 0, tiled=True) for x in listed]
    for c in range(CHUNKS):
        transform, updated = analyse(c, CHUNKS, states[c], sums, operator, transform)
        returned.append(lax.all_to_all(updated, "mem", 0, 0, tiled=True))

    restored = pl.pallas_call(
        functools.partial(scatter_kernel, CHUNKS),
        grid=(lanes,),
        in_specs=[smem] + [block] * CHUNKS,
        out_specs=strip,
        out_shape=jax.ShapeDtypeStruct((rows * band_patches, cells), F),
        compiler_params=params,
        name="scatter",
    )(order, *returned)
    return (restored.reshape(rows, band_patches, cells), transform[None])


def solution(mesh):
    placed = (
        P("mem", "band", None),
        P(),
        P("band", None),
        P("band", None, None),
        P("band", "mem"),
        P("band", "mem", None),
        P("band", "mem", None),
    )
    return jax.shard_map(
        local,
        mesh=mesh,
        in_specs=placed,
        out_specs=(P("mem", "band", None), P("band", "mem", None, None)),
        check_vma=False,
    )
```

```python
import functools
import math

import jax
import jax.numpy as jnp
from jax import lax
from jax.experimental import pallas as pl
from jax.experimental.pallas import tpu as pltpu
from jax.sharding import PartitionSpec as P

F = jnp.float32
BF = jnp.bfloat16
CHUNKS = 2
ANALYSE_VMEM = 40 * 2**20
LANES = 128
VMEM = 56 * 2**20


def split(value, pieces):
    out = []
    for _ in range(pieces):
        head = value.astype(BF)
        out.append(head)
        value = value - head.astype(F)
    return out


def dot(left, right):
    return jnp.dot(left, right, preferred_element_type=F)


def dot_t(left, right):
    return lax.dot_general(left, right, (((1,), (1,)), ((), ())), preferred_element_type=F)


def product(left, right, mul=dot):
    n = left[0].shape[0]
    first = mul(jnp.concatenate(left, axis=0), right[0])
    if len(left) == 2:
        return first[:n] + (first[n:] + mul(left[0], right[1]))
    second = mul(jnp.concatenate(left[:2], axis=0), right[1])
    low = second[n:] + (mul(left[0], right[2]) + first[2 * n :])
    return first[:n] + ((first[n : 2 * n] + second[:n]) + low)


def stacked(left, other, right):
    both = [jnp.concatenate([a, b], axis=0) for a, b in zip(left, other)]
    result = product(both, right)
    n = left[0].shape[0]
    return result[:n], result[n:]


def gather_kernel(chunk, per_worker, order, ens, out):
    workers, per_chunk, rows, _ = out.shape
    patches = ens.shape[0] // rows

    def one(worker, carry):
        for slot in range(per_chunk):
            patch = order[worker * per_worker + chunk * per_chunk + slot]
            out[worker, slot] = ens[pl.ds(patch, rows, stride=patches), :]
        return carry

    lax.fori_loop(0, workers, one, 0, unroll=4)


def scatter_kernel(chunks, order, *refs):
    ins, out = refs[:-1], refs[-1]
    workers, per_chunk, rows, _ = ins[0].shape
    patches = out.shape[0] // rows
    per_worker = per_chunk * chunks

    def one(worker, carry):
        for slot in range(per_worker):
            patch = order[worker * per_worker + slot]
            out[pl.ds(patch, rows, stride=patches), :] = ins[slot // per_chunk][worker, slot % per_chunk]
        return carry

    lax.fori_loop(0, workers, one, 0, unroll=4)


def slots_kernel(count, index, values, precision, out):
    patches, slots = index.shape
    channels = out.shape[2]
    place = lax.broadcasted_iota(jnp.int32, (channels, slots), 0)
    lane = lax.broadcasted_iota(jnp.int32, (1, slots), 1)
    for p in range(patches):
        weight = jnp.where(lane < count[0, p], precision[p : p + 1, :], 0.0)
        rows = split(weight, 3) + split(weight * values[p : p + 1, :], 3)
        rows = jnp.concatenate([row.astype(F) for row in rows] + [jnp.zeros((2, slots), F)], axis=0).astype(BF)
        picker = jnp.where(place == index[p : p + 1, :], 1.0, 0.0).astype(BF)
        sums = dot_t(rows, picker)
        total = sums[0:1] + (sums[1:2] + sums[2:3])
        valued = sums[3:4] + (sums[4:5] + sums[5:6])
        out[p] = jnp.concatenate([total, jnp.sqrt(total), valued, jnp.zeros((5, channels), F)], axis=0)


def double_poly(mats, pieces):
    parts = [split(m, pieces) for m in mats]
    squares = [product(p[:2], p[:2]) for p in parts]
    outer = [split(s, 2) for s in squares]
    inner = [split(0.0625 * s - 0.5625 * m, 2) for s, m in zip(squares, mats)]
    poly = [
        product(o, i) + (1.6875 * s - 2.4375 * m) for o, i, s, m in zip(outer, inner, squares, mats)
    ]
    return parts, poly


def double_step(mats, roots, pieces):
    parts, poly = double_poly(mats, pieces)
    spoly = [split(p, pieces) for p in poly]
    if roots is None:
        size = mats[0].shape[0]
        row = lax.broadcasted_iota(jnp.int32, (size, size), 0)
        col = lax.broadcasted_iota(jnp.int32, (size, size), 1)
        new_roots = [jnp.where(row == col, p + 2.25, p) for p in poly]
        half = [2.25 * m + product(s, p) for m, s, p in zip(mats, parts, spoly)]
    else:
        half, new_roots = [], []
        for m, z, s, p in zip(mats, roots, parts, spoly):
            upper, lower = stacked(s, split(z, 2), p)
            half.append(2.25 * m + upper)
            new_roots.append(2.25 * z + lower)
    new_mats = [2.25 * u + product(split(u, pieces), p) for u, p in zip(half, spoly)]
    return new_mats, new_roots


def analyse_kernel(members, doubles, first, last, state, sums, operator, *refs):
    transform_out, updated_out, transform, leave, updated = (refs + (refs[-3],))[-5:] if last else refs[-5:]
    n = transform.shape[0]
    cells = state.shape[3]
    every = range(n)
    row = lax.broadcasted_iota(jnp.int32, (members, members), 0)
    col = lax.broadcasted_iota(jnp.int32, (members, members), 1)
    inflation = members - 1.0

    oper = split(operator[...], 3)
    mats, traces, projected = [], [], []
    states = [state[:, i].reshape(members, cells) for i in every]
    mapped = [product(split(x, 3), oper) for x in states]
    for i in every:
        mean = jnp.mean(mapped[i], axis=0, keepdims=True)
        pert = mapped[i] - mean
        innov = sums[first + i, 2:3] - mean * sums[first + i, 0:1]
        projected.append(jnp.sum(pert * innov, axis=1, keepdims=True))
        scaled = pert * sums[first + i, 1:2]
        trace = jnp.sum(jnp.sum(scaled * scaled, axis=0, keepdims=True), axis=1, keepdims=True)
        traces.append(trace + inflation * members)
        mats.append(scaled)
    pieces = [split(m, 3) for m in mats]
    grams = [product(p, p, dot_t) for p in pieces]
    mats = [jnp.where(row == col, g + inflation, g) * (1.0 / t) for g, t in zip(grams, traces)]

    mats, roots = double_step(mats, None, 3)
    for _ in range(doubles - 2):
        mats, roots = double_step(mats, roots, 2)
    _, poly = double_poly(mats, 2)
    roots = [2.25 * z + product(split(z, 2), split(p, 2)) for z, p in zip(roots, poly)]

    for i in every:
        root, trace = roots[i], traces[i]
        scale = math.sqrt(inflation) / jnp.sqrt(trace)
        transform[i] = root * scale
        x = state[:, i].reshape(members, cells)
        mean = jnp.mean(x, axis=0, keepdims=True)
        pert = x - mean
        once = jnp.sum(root * projected[i], axis=0, keepdims=True)
        weight = jnp.sum(root * once, axis=1, keepdims=True) / trace
        shift = mean + jnp.sum(pert * weight, axis=0, keepdims=True)
        result = shift + scale * product(split(root, 2), split(pert, 2))
        updated[:, i] = result.reshape(updated.shape[0], updated.shape[2], cells)
    copies = [pltpu.make_async_copy(transform, transform_out.at[pl.ds(first, n)], leave.at[0])]
    if not last:
        copies.append(pltpu.make_async_copy(updated, updated_out, leave.at[1]))
    for copy in copies:
        copy.start()
    for copy in copies:
        copy.wait()


def analyse(chunk, chunks, state, sums, operator, transform):
    workers, per_chunk, rows, cells = state.shape
    members = workers * rows
    anywhere = pl.BlockSpec(memory_space=pl.ANY)
    vmem = pl.BlockSpec(memory_space=pltpu.VMEM)
    first = chunk * per_chunk
    last = chunk == chunks - 1
    in_specs = [vmem, vmem, vmem]
    args = [pltpu.with_memory_space_constraint(state, pltpu.VMEM), sums, operator]
    aliases = {}
    if transform is not None:
        in_specs.append(anywhere)
        args.append(transform)
        aliases = {3: 0}
    return pl.pallas_call(
        functools.partial(analyse_kernel, members, 6, first, last),
        in_specs=in_specs,
        out_specs=[anywhere, vmem if last else anywhere],
        out_shape=[
            jax.ShapeDtypeStruct((per_chunk * chunks, members, members), F),
            pltpu.VMEM(state.shape, F) if last else pltpu.HBM(state.shape, F),
        ],
        scratch_shapes=[pltpu.VMEM((per_chunk, members, members), F), pltpu.SemaphoreType.DMA((2,))]
        + ([] if last else [pltpu.VMEM(state.shape, F)]),
        input_output_aliases=aliases,
        compiler_params=pltpu.CompilerParams(vmem_limit_bytes=ANALYSE_VMEM),
        cost_estimate=pl.CostEstimate(
            flops=per_chunk * 100 * 2 * members**3, bytes_accessed=12 * per_chunk * members**2, transcendentals=0
        ),
        name="analyse",
    )(*args)


def local(ensemble, column_operator, patch_order, obs_index, obs_count, obs_values, obs_precision):
    rows, band_patches, cells = ensemble.shape
    workers = lax.axis_size("mem")
    worker = lax.axis_index("mem")
    per_worker = band_patches // workers
    per_chunk = per_worker // CHUNKS
    levels = column_operator.shape[0]
    columns = cells // levels
    channels = columns * column_operator.shape[1]
    smem = pl.BlockSpec(memory_space=pltpu.SMEM)
    vmem = pl.BlockSpec(memory_space=pltpu.VMEM)
    params = pltpu.CompilerParams(vmem_limit_bytes=VMEM)
    piece = jax.ShapeDtypeStruct((workers, per_chunk, rows, cells), F)
    order = patch_order[0]
    lanes = cells // LANES
    strip = pl.BlockSpec((rows * band_patches, LANES), lambda j: (0, j))
    block = pl.BlockSpec((workers, per_chunk, rows, LANES), lambda j: (0, 0, 0, j))

    listed = [
        pl.pallas_call(
            functools.partial(gather_kernel, c, per_worker),
            grid=(lanes,),
            in_specs=[smem, strip],
            out_specs=block,
            out_shape=piece,
            compiler_params=params,
            cost_estimate=pl.CostEstimate(flops=0, bytes_accessed=2 * ensemble.size * 4, transcendentals=0),
            name="gather",
        )(order, ensemble.reshape(rows * band_patches, cells))
        for c in range(CHUNKS)
    ]

    my_index = lax.dynamic_slice_in_dim(obs_index[0], worker * per_worker, per_worker, 0)
    sums = pl.pallas_call(
        slots_kernel,
        in_specs=[smem, vmem, vmem, vmem],
        out_specs=vmem,
        out_shape=jax.ShapeDtypeStruct((per_worker, 8, channels), F),
        compiler_params=params,
        name="slots",
    )(obs_count, my_index, obs_values[0], obs_precision[0])
    width = column_operator.shape[1]
    operator = jnp.concatenate(
        [jnp.pad(column_operator, ((0, 0), (k * width, channels - (k + 1) * width))) for k in range(columns)]
    )

    transform = None
    returned = []
    states = [lax.all_to_all(x, "mem", 0, 0, tiled=True) for x in listed]
    for c in range(CHUNKS):
        transform, updated = analyse(c, CHUNKS, states[c], sums, operator, transform)
        returned.append(lax.all_to_all(updated, "mem", 0, 0, tiled=True))

    restored = pl.pallas_call(
        functools.partial(scatter_kernel, CHUNKS),
        grid=(lanes,),
        in_specs=[smem] + [block] * CHUNKS,
        out_specs=strip,
        out_shape=jax.ShapeDtypeStruct((rows * band_patches, cells), F),
        compiler_params=params,
        name="scatter",
    )(order, *returned)
    return (restored.reshape(rows, band_patches, cells), transform[None])


def solution(mesh):
    placed = (
        P("mem", "band", None),
        P(),
        P("band", None),
        P("band", None, None),
        P("band", "mem"),
        P("band", "mem", None),
        P("band", "mem", None),
    )
    return jax.shard_map(
        local,
        mesh=mesh,
        in_specs=placed,
        out_specs=(P("mem", "band", None), P("band", "mem", None, None)),
        check_vma=False,
    )
```
